32 devices in a mesh: groups: 2 (over x), row: 16 (over z, y, core).
Axes of the slice: x: 2, y: 2, z: 4, core: 2. Of those that a mesh axis runs over, the one named last changes fastest.
Arguments:
- query_acts: bfloat16 [1024, 14336], P('groups', 'row'), parts along dimension 0, may hold values from -6 to 6
- query_grads: bfloat16 [1024, 8192], P('groups', 'row'), parts along dimension 0, may hold values from -6 to 6
- query_index: int32 [512], P('groups'), parts along dimension 0, may hold values from 0 to 511
- act_basis: bfloat16 [14336, 14336], P('row'), may hold values from -0.0625 to 0.0625
- grad_basis: bfloat16 [8192, 8192], P('row'), may hold values from -0.09375 to 0.09375
- eigenvalues: bfloat16 [8192, 14336], P(None, 'row'), may hold values from 0.019897461 to 4
- train_acts: bfloat16 [512, 14336], P(None, 'row'), may hold values from -1.5 to 1.5
- train_grads: bfloat16 [512, 8192], P(None, 'row'), may hold values from -0.0625 to 0.0625
- train_index: int32 [512], P('groups'), parts along dimension 0, may hold values from 0 to 511
Outputs:
- scores: float32 [512], P(('groups', 'row')), parts along dimension 0
The draws below stay inside these ranges and needn't reach their ends.
There are 2 independent parts, one for each index of `groups`. The reference program is written for one: setup_inputs(seed, part) draws one part's arguments, and reference() takes and returns one part's arrays. A program takes and returns all parts, laid end to end along the dimension named above; an argument that names none is the same for every part. Nothing has to cross between parts.
Inputs may be any that keep to these rules, and one draw needn't show every extreme that they name: `query_index`: rows of the stored query arrays. `train_index`: rows of the stored training arrays.
All inputs are finite; a program needn't handle non-finite values.
Results may differ from the reference program's by a relative error of at most 0.005.
Values may be sent and summed in bfloat16 or wider, within the bound.
A program may use at most 128 MiB of HBM per device.

```python
import math
import jax
import jax.numpy as jnp

D = 8192
FFW = 14336
QTOK = 256
TTOK = 256
QPOOL = 512
TPOOL = 512


def set_ends(result, rng, low, high):
    place = [jax.random.randint(jax.random.fold_in(rng, axis), (), 0, length) for axis, length in enumerate(result.shape)]
    widest = result.shape.index(max(result.shape))
    neighbour = place[:widest] + [(place[widest] + 1) % result.shape[widest]] + place[widest + 1:]
    return result.at[tuple(place)].set(low).at[tuple(neighbour)].set(high)


def raised(result, stream_key, source, target, parts, factor):
    def block_of(dim):
        return (jnp.arange(result.shape[dim]) // (result.shape[dim] // parts)).reshape((-1,) + (1,) * (result.ndim - 1 - dim))

    near = jax.random.permutation(stream_key, parts)[block_of(target)]
    other_side = (block_of(target) + parts // 2) % parts
    return jnp.where((block_of(source) == near) | (block_of(source) == other_side), factor * result, result)


def shard_levels(own_key, dims, shards, low, high):
    gain = 1.0
    for axis_at, parts in shards:
        heights = jax.random.uniform(jax.random.fold_in(jax.random.fold_in(own_key, 6), axis_at), (parts,), jnp.float32, low / len(shards), high / len(shards))
        gain = gain * jnp.repeat(jnp.exp(heights), dims[axis_at] // parts).reshape((-1,) + (1,) * (len(dims) - 1 - axis_at))
    return gain


def bell_draw(own_key, dims, width, most, pieces=(), kind=jnp.bfloat16):
    array = jax.random.normal(own_key, dims, jnp.float32) * width
    if len(pieces) > 0:
        array = shard_levels(own_key, dims, pieces, -0.22, 0.18) * array
    return jnp.clip(array, min=-most, max=most).astype(kind)


def bell_draw_with(rng, dims, deviation, reach, pieces, heavy, held_as=jnp.bfloat16):
    values = deviation * jax.random.normal(rng, dims, jnp.float32)
    if pieces:
        values = values * shard_levels(rng, dims, pieces, -0.22, 0.18)
    return jnp.clip(raised(values, jax.random.fold_in(rng, 3), *heavy), -reach, reach).astype(held_as)


def setup_inputs(seed: int = 0, part: int = 0) -> dict:
    arg_keys = jax.random.split(jax.random.key(seed), 10)
    part_splits = jax.random.split(jax.random.fold_in(arg_keys[9], part), 10)
    query_acts = bell_draw(part_splits[0], (QPOOL, FFW), 1.0, 6.0, ((1, 16),))
    query_grads = bell_draw(part_splits[1], (QPOOL, D), 1.0, 6.0, ((1, 16),))
    query_index = set_ends(jax.random.randint(part_splits[2], (QTOK,), 0, QPOOL), jax.random.fold_in(part_splits[2], 1), 0, QPOOL - 1).astype(jnp.int32)
    act_basis = bell_draw_with(arg_keys[3], (FFW, FFW), FFW ** -0.5, 0.0625, ((0, 16),), (0, 1, 16, 2.0))
    grad_basis = bell_draw_with(arg_keys[4], (D, D), D ** -0.5, 0.09375, ((0, 16),), (0, 1, 16, 2.0))
    eigenvalues = jnp.clip(jnp.exp(math.log(4.0) - 5.3034575 * jax.random.uniform(arg_keys[5], (D, FFW), jnp.float32) ** shard_levels(arg_keys[5], (D, FFW), ((1, 16),), -0.2, 0.2)), 0.019897461, 4.0).astype(jnp.bfloat16)
    train_acts = bell_draw(arg_keys[6], (TPOOL, FFW), 0.25, 1.5, ((1, 16),))
    train_grads = bell_draw(arg_keys[7], (TPOOL, D), D ** -0.5, 0.0625, ((1, 16),))
    train_index = set_ends(jax.random.randint(part_splits[8], (TTOK,), 0, TPOOL), jax.random.fold_in(part_splits[8], 1), 0, TPOOL - 1).astype(jnp.int32)
    return {"query_acts": query_acts, "query_grads": query_grads, "query_index": query_index, "act_basis": act_basis, "grad_basis": grad_basis, "eigenvalues": eigenvalues, "train_acts": train_acts, "train_grads": train_grads, "train_index": train_index}


damping = 0.1


def reference(query_acts, query_grads, query_index, act_basis, grad_basis, eigenvalues, train_acts, train_grads, train_index):
    chosen_acts = jnp.take(query_acts, query_index, axis=0)
    chosen_grads = jnp.take(query_grads, query_index, axis=0)
    rotated_acts = jnp.dot(chosen_acts, act_basis, preferred_element_type=jnp.float32).astype(jnp.bfloat16)
    rotated_grads = jnp.dot(chosen_grads, grad_basis, preferred_element_type=jnp.float32).astype(jnp.bfloat16)
    gradient_tile = jnp.dot(rotated_grads.T, rotated_acts, preferred_element_type=jnp.float32) / QTOK
    scaled_tile = (gradient_tile / (eigenvalues.astype(jnp.float32) + damping)).astype(jnp.bfloat16)
    picked_acts = jnp.take(train_acts, train_index, axis=0)
    picked_grads = jnp.take(train_grads, train_index, axis=0)
    mixed = jnp.dot(picked_grads, scaled_tile, preferred_element_type=jnp.float32)
    return jnp.sum(mixed * picked_acts.astype(jnp.float32), axis=1)
```

```python
import functools

import jax
import jax.numpy as jnp
from jax import lax
from jax.experimental import pallas as pl
from jax.experimental.pallas import tpu as pltpu
from jax.sharding import PartitionSpec as P

damping = 0.1
F32 = jnp.float32
BF16 = jnp.bfloat16
BUFFERS = 3


def flip(r, t):
    d = 1 << t
    return r + d - 2 * d * ((r // d) % 2)


def xor(k, r, bits):
    total = 0
    for t in range(bits):
        d = 1 << t
        total = total + d * (((k // d) % 2 + (r // d) % 2) % 2)
    return total


def zeros_below(k, bits):
    t = 0
    while t < bits and (k >> t) % 2 == 0:
        t += 1
    return t


def pick(index_ref, rows_ref):
    count, pool = index_ref.shape[0], rows_ref.shape[0]
    place = lax.broadcasted_iota(jnp.int32, (count, pool), 1)
    chosen = jnp.where(place == index_ref[...], 1.0, 0.0).astype(BF16)
    return jnp.dot(chosen, rows_ref[...], preferred_element_type=F32)


class Reduce:
    def __init__(self, r, n, bits, basis, chosen, buf, buf_sem, snd, rcv, near_snd, near, send_sem, recv_sem):
        self.__dict__.update(locals())

    def slot(self, s):
        n, quarter = self.n, self.n // 4
        first, last = (n - 1 - s) // (n - 1), s // (n - 1)
        odd = s % 2 - last + first
        p = odd * ((s + 1) // 2) + (1 - odd) * (s // 2 - 1 + last)
        return 4 * (quarter - 1 - p % quarter) + 2 * (1 - p // quarter) + odd

    def fetch(self, s):
        width, depth = self.snd.shape[2], self.basis.shape[0]
        b = xor(self.slot(s), self.r, self.bits)
        return pltpu.make_async_copy(
            self.basis.at[:, pl.ds(pl.multiple_of(b * width, 128), width)],
            self.buf.at[s % BUFFERS, pl.ds(0, depth)],
            self.buf_sem.at[s % BUFFERS],
        )

    def copy(self, k, t):
        snd, rcv = (self.near_snd, self.near) if t == 0 else (self.snd, self.rcv)
        return pltpu.make_async_remote_copy(
            src_ref=snd.at[k // 2],
            dst_ref=rcv.at[k // 2],
            send_sem=self.send_sem.at[k],
            recv_sem=self.recv_sem.at[k],
            device_id={"row": flip(self.r, t)},
            device_id_type=pl.DeviceIdType.MESH,
        )

    def prefetch(self):
        for s in range(BUFFERS):
            self.fetch(s).start()

    def product(self, s):
        depth = self.basis.shape[0]
        self.fetch(s).wait()
        return jnp.dot(
            self.chosen[...], self.buf[s % BUFFERS, pl.ds(0, depth)], preferred_element_type=F32
        )

    def after(self, s):
        @pl.when(s + BUFFERS < self.n)
        def _():
            self.fetch(s + BUFFERS).start()

    def total(self, k, t):
        value = self.near[k // 2]
        for u in range(1, t):
            self.copy(k + (1 << u), u).wait_recv()
            value = value + self.rcv[(k + (1 << u)) // 2].astype(F32)
        return value

    def send(self, k, t):
        self.snd[k // 2] = self.total(k, t).astype(BF16)
        self.copy(k, t).start()

    def give(self, s):
        k = self.slot(s)
        self.near_snd[k // 2] = self.product(s)
        self.copy(k, 0).start()
        self.after(s)

    def keep(self, s):
        k = self.slot(s)
        value = self.product(s)
        self.copy(k + 1, 0).wait_recv()
        self.near[k // 2] = self.near[k // 2] + value
        self.after(s)

    def products(self):
        self.give(0)

        def body(p, carry):
            self.give(2 * p - 1)
            self.keep(2 * p)

            @pl.when(p - 1 < self.n // 4)
            def _():
                self.send(self.slot(2 * p), 1)

            return carry

        lax.fori_loop(1, self.n // 2, body, 0)
        self.keep(self.n - 1)

    def finish(self):
        def body(p, carry):
            self.copy(2 * p + 1, 0).wait_send()

            @pl.when(p > 0)
            def _():
                self.copy(2 * p, 1).wait_send()

            return carry

        lax.fori_loop(0, self.n // 2, body, 0)


class Gather:
    def __init__(self, r, n, bits, slots, send_sem, recv_sem):
        self.__dict__.update(locals())

    def copy(self, j, t):
        k = j + (1 << t)
        return pltpu.make_async_remote_copy(
            src_ref=self.slots.at[j],
            dst_ref=self.slots.at[k],
            send_sem=self.send_sem.at[k],
            recv_sem=self.recv_sem.at[k],
            device_id={"row": flip(self.r, t)},
            device_id_type=pl.DeviceIdType.MESH,
        )

    def wait(self, k, t):
        self.copy(k - (1 << t), t).wait_recv()

    def arrive(self, j):
        top = zeros_below(j, self.bits)
        if j > 0:
            self.wait(j, top)
        for t in reversed(range(top)):
            self.copy(j, t).start()

    def finish(self):
        def body(k, carry):
            self.copy(k - 1, 0).wait_send()
            return carry

        lax.fori_loop(1, self.n, body, 0)


def kernel(
    n,
    bits,
    query_index,
    train_index,
    query_acts,
    query_grads,
    train_acts,
    train_grads,
    act_basis,
    grad_basis,
    eigenvalues,
    out,
    chosen_acts,
    chosen_grads,
    picked_acts,
    rotated,
    rotated_rest,
    mixed,
    act_buf,
    grad_buf,
    act_snd,
    act_rcv,
    act_near_snd,
    act_near,
    grad_snd,
    grad_rcv,
    grad_near_snd,
    grad_near,
    grad_all,
    train_all,
    score,
    score_in,
    act_buf_sem,
    grad_buf_sem,
    act_send,
    act_recv,
    grad_send,
    grad_recv,
    gall_send,
    gall_recv,
    tall_send,
    tall_recv,
    score_send,
    score_recv,
):
    r = lax.axis_index("row")
    quarter = n // 4
    acts = Reduce(
        r, n, bits, act_basis, chosen_acts, act_buf, act_buf_sem,
        act_snd, act_rcv, act_near_snd, act_near, act_send, act_recv,
    )
    grads = Reduce(
        r, n, bits, grad_basis, chosen_grads, grad_buf, grad_buf_sem,
        grad_snd, grad_rcv, grad_near_snd, grad_near, grad_send, grad_recv,
    )
    whole = Gather(r, n, bits, grad_all, gall_send, gall_recv)
    train = Gather(r, n, bits, train_all, tall_send, tall_recv)
    query_count = query_index.shape[0]

    grads.prefetch()
    acts.prefetch()
    barrier = pltpu.get_barrier_semaphore()
    for k in range(1, n):
        pl.semaphore_signal(
            barrier, inc=1, device_id={"row": lax.rem(r + k, n)},
            device_id_type=pl.DeviceIdType.MESH,
        )
    train_all[0] = pick(train_index, train_grads).astype(BF16)
    chosen_grads[...] = pick(query_index, query_grads).astype(BF16)
    pl.semaphore_wait(barrier, n - 1)

    train.arrive(0)
    grads.products()
    chosen_acts[...] = pick(query_index, query_acts).astype(BF16)
    acts.products()
    picked_acts[...] = pick(train_index, train_acts).astype(BF16)

    rows = eigenvalues.shape[0] // n

    def order(s):
        m, low = s % quarter, s // quarter
        high = 0
        for t in range(bits - 2):
            high = high + ((m // (1 << t)) % 2) * (1 << (bits - 3 - t))
        return 4 * high + low

    def fetch(s):
        b = xor(order(s), r, bits)
        return pltpu.make_async_copy(
            eigenvalues.at[pl.ds(pl.multiple_of(b * rows, 16), rows)],
            act_buf.at[s % BUFFERS, pl.ds(0, rows)],
            act_buf_sem.at[s % BUFFERS],
        )

    for s in range(BUFFERS):
        fetch(s).start()
    mixed[...] = jnp.zeros_like(mixed)

    fours = [order(s) for s in range(quarter)]
    for k in fours[1:]:
        train.arrive(k)
    for k in reversed(range(4, n, 4)):
        grads.send(k, zeros_below(k, bits))
    grad_all[0] = grads.total(0, bits).T.astype(BF16)
    whole.arrive(0)
    for k, j in zip(reversed(range(4, n, 4)), fours[1:]):
        acts.send(k, zeros_below(k, bits))
        whole.arrive(j)
    own_acts = acts.total(0, bits)
    rotated[...] = own_acts.astype(BF16)
    rotated_rest[...] = (own_acts - rotated[...].astype(F32)).astype(BF16)

    def body(s, carry):
        k = order(s)
        low = s // quarter

        @pl.when(low == 2)
        def _():
            for g in (train, whole):
                g.wait(k, 1)
                g.copy(k, 0).start()

        @pl.when(low % 2 == 1)
        def _():
            for g in (train, whole):
                g.wait(k, 0)

        tile = jnp.dot(grad_all[k], rotated[...], preferred_element_type=F32)
        tile += jnp.dot(grad_all[k], rotated_rest[...], preferred_element_type=F32)
        fetch(s).wait()
        level = (act_buf[s % BUFFERS, pl.ds(0, rows)].astype(F32) + damping) * query_count
        exact = tile / level
        scaled = exact.astype(BF16)
        rest = (exact - scaled.astype(F32)).astype(BF16)
        mixed[...] += jnp.dot(train_all[k], scaled, preferred_element_type=F32) + jnp.dot(
            train_all[k], rest, preferred_element_type=F32
        )

        @pl.when(s + BUFFERS < n)
        def _():
            fetch(s + BUFFERS).start()

        return carry

    lax.fori_loop(0, n, body, 0)

    terms = mixed[...] * picked_acts[...].astype(F32)
    lanes = terms[:, :128]
    for c in range(1, terms.shape[1] // 128):
        lanes = lanes + terms[:, c * 128 : (c + 1) * 128]
    score[...] = lanes
    tokens = out.shape[0]

    def score_copy(k):
        to = lax.rem(r + k, n)
        return pltpu.make_async_remote_copy(
            src_ref=score.at[pl.ds(pl.multiple_of(to * tokens, 8), tokens)],
            dst_ref=score_in.at[k],
            send_sem=score_send.at[k],
            recv_sem=score_recv.at[k],
            device_id={"row": to},
            device_id_type=pl.DeviceIdType.MESH,
        )

    for k in range(1, n):
        score_copy(k).start()
    result = score[pl.ds(pl.multiple_of(r * tokens, 8), tokens)]
    for k in range(1, n):
        score_copy(k).wait_recv()
        result = result + score_in[k]
    out[...] = jnp.sum(result, axis=1, keepdims=True)

    for part in (acts, grads, whole, train):
        part.finish()
    for k in range(1, n):
        score_copy(k).wait_send()


def fused(
    n,
    query_acts,
    query_grads,
    query_index,
    act_basis,
    grad_basis,
    eigenvalues,
    train_acts,
    train_grads,
    train_index,
):
    bits = n.bit_length() - 1
    q, t = query_index.shape[0], train_index.shape[0]
    wa, wg = query_acts.shape[1], query_grads.shape[1]
    vmem = pl.BlockSpec(memory_space=pltpu.VMEM)
    hbm = pl.BlockSpec(memory_space=pl.ANY)
    dma = pltpu.SemaphoreType.DMA
    scratch = [
        pltpu.VMEM((q, wa), BF16),
        pltpu.VMEM((q, wg), BF16),
        pltpu.VMEM((t, wa), BF16),
        pltpu.VMEM((q, wa), BF16),
        pltpu.VMEM((q, wa), BF16),
        pltpu.VMEM((t, wa), F32),
        pltpu.VMEM((BUFFERS, max(wa, wg), wa), BF16),
        pltpu.VMEM((BUFFERS, wg, wg), BF16),
        pltpu.VMEM((n // 2, q, wa), BF16),
        pltpu.VMEM((n // 2, q, wa), BF16),
        pltpu.VMEM((n // 2, q, wa), F32),
        pltpu.VMEM((n // 2, q, wa), F32),
        pltpu.VMEM((n // 2, q, wg), BF16),
        pltpu.VMEM((n // 2, q, wg), BF16),
        pltpu.VMEM((n // 2, q, wg), F32),
        pltpu.VMEM((n // 2, q, wg), F32),
        pltpu.VMEM((n, wg, q), BF16),
        pltpu.VMEM((n, t, wg), BF16),
        pltpu.VMEM((t, 128), F32),
        pltpu.VMEM((n, t // n, 128), F32),
        dma((BUFFERS,)),
        dma((BUFFERS,)),
    ] + [dma((n,)) for _ in range(10)]
    flops = 2 * n * (q * wa * wa + q * wg * wg + q * wa * wg + t * wa * wg)
    moved = 2 * (act_basis.size + grad_basis.size + eigenvalues.size)
    scores = pl.pallas_call(
        functools.partial(kernel, n, bits),
        out_shape=jax.ShapeDtypeStruct((t // n, 1), F32),
        in_specs=[vmem] * 6 + [hbm] * 3,
        out_specs=vmem,
        scratch_shapes=scratch,
        compiler_params=pltpu.CompilerParams(
            collective_id=0, has_side_effects=True, vmem_limit_bytes=64 * 1024 * 1024 - 256 * 1024
        ),
        cost_estimate=pl.CostEstimate(flops=flops, bytes_accessed=moved, transcendentals=0),
        name="influence",
    )(
        query_index.reshape(q, 1),
        train_index.reshape(t, 1),
        query_acts,
        query_grads,
        train_acts,
        train_grads,
        act_basis,
        grad_basis,
        eigenvalues,
    )
    return scores.reshape(t // n)


def plain(
    query_acts,
    query_grads,
    query_index,
    act_basis,
    grad_basis,
    eigenvalues,
    train_acts,
    train_grads,
    train_index,
):
    chosen_acts = jnp.take(query_acts, query_index, axis=0)
    chosen_grads = jnp.take(query_grads, query_index, axis=0)
    picked_acts = jnp.take(train_acts, train_index, axis=0)
    picked_grads = jnp.take(train_grads, train_index, axis=0)
    whole_picked = lax.all_gather(picked_grads, "row", axis=1, tiled=True)
    rotated_grads = lax.psum_scatter(
        jnp.dot(chosen_grads, grad_basis, preferred_element_type=F32),
        "row", scatter_dimension=1, tiled=True,
    ).astype(BF16)
    rotated_acts = lax.psum_scatter(
        jnp.dot(chosen_acts, act_basis, preferred_element_type=F32),
        "row", scatter_dimension=1, tiled=True,
    ).astype(BF16)
    whole_grads = lax.all_gather(rotated_grads, "row", axis=1, tiled=True)
    tile = lax.dot_general(
        whole_grads, rotated_acts, (((0,), (0,)), ((), ())), preferred_element_type=F32
    )
    level = (eigenvalues.astype(F32) + damping) * query_index.shape[0]
    mixed = jnp.dot(whole_picked, (tile / level).astype(BF16), preferred_element_type=F32)
    partial_scores = jnp.sum(mixed * picked_acts.astype(F32), axis=1)
    return lax.psum_scatter(partial_scores, "row", scatter_dimension=0, tiled=True)


def solution(mesh):
    n = mesh.shape["row"]
    placed = (
        P("groups", "row"),
        P("groups", "row"),
        P("groups"),
        P("row", None),
        P("row", None),
        P(None, "row"),
        P(None, "row"),
        P(None, "row"),
        P("groups"),
    )

    def on_device(*arrays):
        wa, wg, t = arrays[0].shape[1], arrays[1].shape[1], arrays[8].shape[0]
        fits = n >= 8 and n & (n - 1) == 0
        fits = fits and wa % 128 == 0 and wg % 128 == 0 and t % (8 * n) == 0
        return fused(n, *arrays) if fits else plain(*arrays)

    return jax.shard_map(
        on_device, mesh=mesh, in_specs=placed, out_specs=P(("groups", "row")), check_vma=False
    )
```

```python
import functools

import jax
import jax.numpy as jnp
from jax import lax
from jax.experimental import pallas as pl
from jax.experimental.pallas import tpu as pltpu
from jax.sharding import PartitionSpec as P

damping = 0.1
F32 = jnp.float32
BF16 = jnp.bfloat16
BUFFERS = 3


def flip(r, t):
    d = 1 << t
    return r + d - 2 * d * ((r // d) % 2)


def xor(k, r, bits):
    total = 0
    for t in range(bits):
        d = 1 << t
        total = total + d * (((k // d) % 2 + (r // d) % 2) % 2)
    return total


def zeros_below(k, bits):
    t = 0
    while t < bits and (k >> t) % 2 == 0:
        t += 1
    return t


def pick(index_ref, rows_ref):
    count, pool = index_ref.shape[1], rows_ref.shape[0]
    place = lax.broadcasted_iota(jnp.int32, (pool, count), 0)
    chosen = jnp.where(place == index_ref[...], 1.0, 0.0).astype(BF16)
    return lax.dot_general(
        chosen, rows_ref[...], (((0,), (0,)), ((), ())), preferred_element_type=F32
    )


class Reduce:
    def __init__(self, r, n, bits, basis, chosen, buf, buf_sem, snd, rcv, near_snd, near, send_sem, recv_sem):
        self.__dict__.update(locals())

    def slot(self, s):
        n, quarter = self.n, self.n // 4
        first, last = (n - 1 - s) // (n - 1), s // (n - 1)
        odd = s % 2 - last + first
        p = odd * ((s + 1) // 2) + (1 - odd) * (s // 2 - 1 + last)
        return 4 * (quarter - 1 - p % quarter) + 2 * (1 - p // quarter) + odd

    def fetch(self, s):
        width, depth = self.snd.shape[2], self.basis.shape[0]
        b = xor(self.slot(s), self.r, self.bits)
        return pltpu.make_async_copy(
            self.basis.at[:, pl.ds(pl.multiple_of(b * width, 128), width)],
            self.buf.at[s % BUFFERS, pl.ds(0, depth)],
            self.buf_sem.at[s % BUFFERS],
        )

    def copy(self, k, t):
        snd, rcv = (self.near_snd, self.near) if t == 0 else (self.snd, self.rcv)
        return pltpu.make_async_remote_copy(
            src_ref=snd.at[k // 2],
            dst_ref=rcv.at[k // 2],
            send_sem=self.send_sem.at[k],
            recv_sem=self.recv_sem.at[k],
            device_id={"row": flip(self.r, t)},
            device_id_type=pl.DeviceIdType.MESH,
        )

    def prefetch(self):
        for s in range(BUFFERS):
            self.fetch(s).start()

    def product(self, s):
        depth = self.basis.shape[0]
        self.fetch(s).wait()
        return jnp.dot(
            self.chosen[...], self.buf[s % BUFFERS, pl.ds(0, depth)], preferred_element_type=F32
        )

    def after(self, s):
        @pl.when(s + BUFFERS < self.n)
        def _():
            self.fetch(s + BUFFERS).start()

    def total(self, k, t):
        value = self.near[k // 2]
        for u in range(1, t):
            self.copy(k + (1 << u), u).wait_recv()
            value = value + self.rcv[(k + (1 << u)) // 2].astype(F32)
        return value

    def send(self, k, t):
        self.snd[k // 2] = self.total(k, t).astype(BF16)
        self.copy(k, t).start()

    def give(self, s):
        k = self.slot(s)
        self.near_snd[k // 2] = self.product(s)
        self.copy(k, 0).start()
        self.after(s)

    def keep(self, s):
        k = self.slot(s)
        value = self.product(s)
        self.copy(k + 1, 0).wait_recv()
        self.near[k // 2] = self.near[k // 2] + value
        self.after(s)

    def products(self, hooks=()):
        self.give(0)

        def body(p, carry):
            self.give(2 * p - 1)
            self.keep(2 * p)

            @pl.when(p - 1 < self.n // 4)
            def _():
                self.send(self.slot(2 * p), 1)

            for step, act in hooks:
                pl.when(p == step)(act)
            return carry

        lax.fori_loop(1, self.n // 2, body, 0)
        self.keep(self.n - 1)

    def finish(self):
        def body(p, carry):
            self.copy(2 * p + 1, 0).wait_send()

            @pl.when(p > 0)
            def _():
                self.copy(2 * p, 1).wait_send()

            return carry

        lax.fori_loop(0, self.n // 2, body, 0)


class Gather:
    def __init__(self, r, n, bits, slots, send_sem, recv_sem):
        self.__dict__.update(locals())

    def copy(self, j, t):
        k = j + (1 << t)
        return pltpu.make_async_remote_copy(
            src_ref=self.slots.at[j],
            dst_ref=self.slots.at[k],
            send_sem=self.send_sem.at[k],
            recv_sem=self.recv_sem.at[k],
            device_id={"row": flip(self.r, t)},
            device_id_type=pl.DeviceIdType.MESH,
        )

    def wait(self, k, t):
        self.copy(k - (1 << t), t).wait_recv()

    def arrive(self, j):
        top = zeros_below(j, self.bits)
        if j > 0:
            self.wait(j, top)
        for t in reversed(range(top)):
            self.copy(j, t).start()

    def finish(self):
        def body(k, carry):
            self.copy(k - 1, 0).wait_send()
            return carry

        lax.fori_loop(1, self.n, body, 0)


def kernel(
    n,
    bits,
    query_index,
    train_index,
    query_acts,
    query_grads,
    train_acts,
    train_grads,
    act_basis,
    grad_basis,
    eigenvalues,
    out,
    chosen_acts,
    chosen_grads,
    picked_acts,
    rotated,
    rotated_rest,
    mixed,
    act_buf,
    grad_buf,
    act_snd,
    act_rcv,
    act_near_snd,
    act_near,
    grad_snd,
    grad_rcv,
    grad_near_snd,
    grad_near,
    grad_all,
    train_all,
    score,
    score_in,
    act_buf_sem,
    grad_buf_sem,
    act_send,
    act_recv,
    grad_send,
    grad_recv,
    gall_send,
    gall_recv,
    tall_send,
    tall_recv,
    score_send,
    score_recv,
):
    r = lax.axis_index("row")
    quarter = n // 4
    acts = Reduce(
        r, n, bits, act_basis, chosen_acts, act_buf, act_buf_sem,
        act_snd, act_rcv, act_near_snd, act_near, act_send, act_recv,
    )
    grads = Reduce(
        r, n, bits, grad_basis, chosen_grads, grad_buf, grad_buf_sem,
        grad_snd, grad_rcv, grad_near_snd, grad_near, grad_send, grad_recv,
    )
    whole = Gather(r, n, bits, grad_all, gall_send, gall_recv)
    train = Gather(r, n, bits, train_all, tall_send, tall_recv)
    query_count = query_index.shape[1]

    def order(s):
        m, low = s % quarter, s // quarter
        high = 0
        for t in range(bits - 2):
            high = high + ((m // (1 << t)) % 2) * (1 << (bits - 3 - t))
        return 4 * high + low

    grads.prefetch()
    acts.prefetch()
    barrier = pltpu.get_barrier_semaphore()
    for k in range(1, n):
        pl.semaphore_signal(
            barrier, inc=1, device_id={"row": lax.rem(r + k, n)},
            device_id_type=pl.DeviceIdType.MESH,
        )
    train_all[0] = pick(train_index, train_grads).astype(BF16)
    chosen_grads[...] = pick(query_index, query_grads).astype(BF16)
    pl.semaphore_wait(barrier, n - 1)

    train.arrive(0)
    grads.products()
    chosen_acts[...] = pick(query_index, query_acts).astype(BF16)
    rows = eigenvalues.shape[0] // n
    fours = [order(s) for s in range(quarter)]
    last = n // 2 - 2

    def spread():
        grad_all[0] = grads.total(0, bits).T.astype(BF16)
        whole.arrive(0)

    hooks = []
    for i, k in enumerate(reversed(range(4, n, 4))):
        hooks.append((min(2 + i, last), functools.partial(grads.send, k, zeros_below(k, bits))))
    hooks.append((last, spread))
    for i, k in enumerate(fours[1:]):
        hooks.append((min(quarter + 1 + i, last + 1), functools.partial(train.arrive, k)))
    acts.products(hooks)
    picked_acts[...] = pick(train_index, train_acts).astype(BF16)

    def fetch(s):
        b = xor(order(s), r, bits)
        return pltpu.make_async_copy(
            eigenvalues.at[pl.ds(pl.multiple_of(b * rows, 16), rows)],
            act_buf.at[s % BUFFERS, pl.ds(0, rows)],
            act_buf_sem.at[s % BUFFERS],
        )

    for s in range(BUFFERS):
        fetch(s).start()
    mixed[...] = jnp.zeros_like(mixed)

    for k, j in zip(reversed(range(4, n, 4)), fours[1:]):
        acts.send(k, zeros_below(k, bits))
        whole.arrive(j)
    own_acts = acts.total(0, bits)
    rotated[...] = own_acts.astype(BF16)
    rotated_rest[...] = (own_acts - rotated[...].astype(F32)).astype(BF16)

    def body(s, carry):
        k = order(s)
        low = s // quarter

        @pl.when(low == 2)
        def _():
            for g in (train, whole):
                g.wait(k, 1)
                g.copy(k, 0).start()

        @pl.when(low % 2 == 1)
        def _():
            for g in (train, whole):
                g.wait(k, 0)

        tile = jnp.dot(grad_all[k], rotated[...], preferred_element_type=F32)
        tile += jnp.dot(grad_all[k], rotated_rest[...], preferred_element_type=F32)
        fetch(s).wait()
        level = (act_buf[s % BUFFERS, pl.ds(0, rows)].astype(F32) + damping) * query_count
        exact = tile / level
        scaled = exact.astype(BF16)
        rest = (exact - scaled.astype(F32)).astype(BF16)
        mixed[...] += jnp.dot(train_all[k], scaled, preferred_element_type=F32) + jnp.dot(
            train_all[k], rest, preferred_element_type=F32
        )

        @pl.when(s + BUFFERS < n)
        def _():
            fetch(s + BUFFERS).start()

        return carry

    lax.fori_loop(0, n, body, 0)

    terms = mixed[...] * picked_acts[...].astype(F32)
    lanes = terms[:, :128]
    for c in range(1, terms.shape[1] // 128):
        lanes = lanes + terms[:, c * 128 : (c + 1) * 128]
    score[...] = lanes
    tokens = out.shape[0]

    def score_copy(k):
        to = lax.rem(r + k, n)
        return pltpu.make_async_remote_copy(
            src_ref=score.at[pl.ds(pl.multiple_of(to * tokens, 8), tokens)],
            dst_ref=score_in.at[k],
            send_sem=score_send.at[k],
            recv_sem=score_recv.at[k],
            device_id={"row": to},
            device_id_type=pl.DeviceIdType.MESH,
        )

    for k in range(1, n):
        score_copy(k).start()
    result = score[pl.ds(pl.multiple_of(r * tokens, 8), tokens)]
    for k in range(1, n):
        score_copy(k).wait_recv()
        result = result + score_in[k]
    out[...] = jnp.sum(result, axis=1, keepdims=True)

    for part in (acts, grads, whole, train):
        part.finish()
    for k in range(1, n):
        score_copy(k).wait_send()


def fused(
    n,
    query_acts,
    query_grads,
    query_index,
    act_basis,
    grad_basis,
    eigenvalues,
    train_acts,
    train_grads,
    train_index,
):
    bits = n.bit_length() - 1
    q, t = query_index.shape[0], train_index.shape[0]
    wa, wg = query_acts.shape[1], query_grads.shape[1]
    vmem = pl.BlockSpec(memory_space=pltpu.VMEM)
    hbm = pl.BlockSpec(memory_space=pl.ANY)
    dma = pltpu.SemaphoreType.DMA
    scratch = [
        pltpu.VMEM((q, wa), BF16),
        pltpu.VMEM((q, wg), BF16),
        pltpu.VMEM((t, wa), BF16),
        pltpu.VMEM((q, wa), BF16),
        pltpu.VMEM((q, wa), BF16),
        pltpu.VMEM((t, wa), F32),
        pltpu.VMEM((BUFFERS, max(wa, wg), wa), BF16),
        pltpu.VMEM((BUFFERS, wg, wg), BF16),
        pltpu.VMEM((n // 2, q, wa), BF16),
        pltpu.VMEM((n // 2, q, wa), BF16),
        pltpu.VMEM((n // 2, q, wa), F32),
        pltpu.VMEM((n // 2, q, wa), F32),
        pltpu.VMEM((n // 2, q, wg), BF16),
        pltpu.VMEM((n // 2, q, wg), BF16),
        pltpu.VMEM((n // 2, q, wg), F32),
        pltpu.VMEM((n // 2, q, wg), F32),
        pltpu.VMEM((n, wg, q), BF16),
        pltpu.VMEM((n, t, wg), BF16),
        pltpu.VMEM((t, 128), F32),
        pltpu.VMEM((n, t // n, 128), F32),
        dma((BUFFERS,)),
        dma((BUFFERS,)),
    ] + [dma((n,)) for _ in range(10)]
    flops = 2 * n * (q * wa * wa + q * wg * wg + q * wa * wg + t * wa * wg)
    moved = 2 * (act_basis.size + grad_basis.size + eigenvalues.size)
    scores = pl.pallas_call(
        functools.partial(kernel, n, bits),
        out_shape=jax.ShapeDtypeStruct((t // n, 1), F32),
        in_specs=[vmem] * 6 + [hbm] * 3,
        out_specs=vmem,
        scratch_shapes=scratch,
        compiler_params=pltpu.CompilerParams(
            collective_id=0, has_side_effects=True, vmem_limit_bytes=64 * 1024 * 1024 - 256 * 1024
        ),
        cost_estimate=pl.CostEstimate(flops=flops, bytes_accessed=moved, transcendentals=0),
        name="influence",
    )(
        query_index.reshape(1, q),
        train_index.reshape(1, t),
        query_acts,
        query_grads,
        train_acts,
        train_grads,
        act_basis,
        grad_basis,
        eigenvalues,
    )
    return scores.reshape(t // n)


def plain(
    query_acts,
    query_grads,
    query_index,
    act_basis,
    grad_basis,
    eigenvalues,
    train_acts,
    train_grads,
    train_index,
):
    chosen_acts = jnp.take(query_acts, query_index, axis=0)
    chosen_grads = jnp.take(query_grads, query_index, axis=0)
    picked_acts = jnp.take(train_acts, train_index, axis=0)
    picked_grads = jnp.take(train_grads, train_index, axis=0)
    whole_picked = lax.all_gather(picked_grads, "row", axis=1, tiled=True)
    rotated_grads = lax.psum_scatter(
        jnp.dot(chosen_grads, grad_basis, preferred_element_type=F32),
        "row", scatter_dimension=1, tiled=True,
    ).astype(BF16)
    rotated_acts = lax.psum_scatter(
        jnp.dot(chosen_acts, act_basis, preferred_element_type=F32),
        "row", scatter_dimension=1, tiled=True,
    ).astype(BF16)
    whole_grads = lax.all_gather(rotated_grads, "row", axis=1, tiled=True)
    tile = lax.dot_general(
        whole_grads, rotated_acts, (((0,), (0,)), ((), ())), preferred_element_type=F32
    )
    level = (eigenvalues.astype(F32) + damping) * query_index.shape[0]
    mixed = jnp.dot(whole_picked, (tile / level).astype(BF16), preferred_element_type=F32)
    partial_scores = jnp.sum(mixed * picked_acts.astype(F32), axis=1)
    return lax.psum_scatter(partial_scores, "row", scatter_dimension=0, tiled=True)


def solution(mesh):
    n = mesh.shape["row"]
    placed = (
        P("groups", "row"),
        P("groups", "row"),
        P("groups"),
        P("row", None),
        P("row", None),
        P(None, "row"),
        P(None, "row"),
        P(None, "row"),
        P("groups"),
    )

    def on_device(*arrays):
        wa, wg, t = arrays[0].shape[1], arrays[1].shape[1], arrays[8].shape[0]
        fits = n >= 8 and n & (n - 1) == 0
        fits = fits and wa % 128 == 0 and wg % 128 == 0 and t % (8 * n) == 0
        return fused(n, *arrays) if fits else plain(*arrays)

    return jax.shard_map(
        on_device, mesh=mesh, in_specs=placed, out_specs=P(("groups", "row")), check_vma=False
    )
```
